512 devices in a mesh: pipe: 4 (over z_hi), dp: 8 (over y, core), tensor: 16 (over z_lo, x).
Axes of the slice: x: 4, y: 4, z: 16 (z_hi: 4, z_lo: 4; z = z_hi * 4 + z_lo), core: 2. Of those that a mesh axis runs over, the one named last changes fastest.
Arguments:
- x_prev: float32 [4, 2, 384, 6144], P('pipe', None, 'tensor', 'dp'), may hold values from -6 to 6
- hid_cot: bfloat16 [4, 2, 384, 24576], P('pipe', None, 'dp', 'tensor'), may hold values from -1.1953125 to 1.1953125
- w_up: bfloat16 [4, 6144, 24576], P('pipe', 'dp', 'tensor'), may hold values from -0.078125 to 0.078125
Outputs:
- upstream_grad: bfloat16 [4, 2, 384, 6144], P('pipe', None, 'tensor', 'dp')
- grad_up: bfloat16 [4, 6144, 24576], P('pipe', 'dp', 'tensor')
The draws below stay inside these ranges and needn't reach their ends.
All inputs are finite; a program needn't handle non-finite values. Where the reference program divides by a largest or mean magnitude, that divisor is 1e-20 or more.
Results may differ from the reference program's by a relative error of at most 0.03.
Values may be sent and summed in bfloat16 or wider, within the bound.
No kernel may reach another device: no remote copies, remote signals or barrier semaphores. Data moves between devices by JAX's collectives and lax.ppermute only.
A program may use at most 64 MiB of HBM per device.

```python
import jax
import jax.numpy as jnp
from jax import lax

D = 6144
F_DEV = 1536
BLOCK = 128
MICRO = 2
SECTIONS = 4
TOKENS = 384
FF = 24576
DB = 768
N_DP = 8
N_TENSOR = 16


def steps_of(key, extent, shards, least, high):
    factor_of, own = 1.0, jax.random.fold_in(key, 6)
    for axis_at, shards_of in shards:
        draws = jnp.exp(jax.random.uniform(jax.random.fold_in(own, axis_at), (shards_of,), jnp.float32, least / len(shards), high / len(shards)))
        factor_of = factor_of * jnp.repeat(draws, extent[axis_at] // shards_of).reshape([-1 if axis == axis_at else 1 for axis in range(len(extent))])
    return factor_of


def noise(stream_key, dims, spread, bound, pieces=(), kind=jnp.bfloat16):
    drawn = spread * jax.random.normal(stream_key, dims, jnp.float32)
    if pieces:
        drawn = drawn * steps_of(stream_key, dims, pieces, -0.22, 0.18)
    return jnp.clip(drawn, -bound, bound).astype(kind)


def setup_inputs(seed: int = 0) -> dict:
    streams_of = jax.random.split(jax.random.key(seed), 4)
    return {
        "x_prev": noise(streams_of[0], (SECTIONS, MICRO, TOKENS, D), 1.0, 6.0, ((0, 4), (2, 16), (3, 8)), jnp.float32),
        "hid_cot": noise(streams_of[1], (SECTIONS, MICRO, TOKENS, FF), 0.2, 1.1953125, ((0, 4), (2, 8), (3, 16))),
        "w_up": noise(streams_of[2], (SECTIONS, D, FF), D ** -0.5, 0.078125, ((0, 4), (1, 8), (2, 16))),
    }


eps_scale = 1e-6
gelu_coef = 0.7978845608028654
cubic_coef = 0.044715


def gelu_slope(preact):
    tanh_arg = gelu_coef * (preact + cubic_coef * preact * preact * preact)
    tangent = jnp.tanh(tanh_arg)
    return 0.5 * (1.0 + tangent) + 0.5 * preact * (1.0 - tangent * tangent) * gelu_coef * (1.0 + 3.0 * cubic_coef * preact * preact)


def rounded(values):
    return lax.optimization_barrier(values.astype(jnp.bfloat16)).astype(jnp.float32)


def reference(x_prev, hid_cot, w_up):
    blocks = x_prev.reshape(SECTIONS, MICRO, TOKENS, D // BLOCK, BLOCK)
    block_scale = (jnp.max(jnp.abs(blocks), axis=-1, keepdims=True) + eps_scale).astype(jnp.bfloat16)
    coded_vals = (blocks / block_scale.astype(jnp.float32)).astype(jnp.bfloat16)
    restored = (coded_vals.astype(jnp.float32) * block_scale.astype(jnp.float32)).astype(jnp.bfloat16)
    received = jnp.roll(restored.reshape(SECTIONS, MICRO, TOKENS, D), 1, axis=0)

    def section_grads(operands):
        features, cotangent, up_matrix = operands

        def block_sum(carry, group):
            first = group * DB
            feat_cols = lax.dynamic_slice_in_dim(features, first, DB, 2)
            matrix_rows = lax.dynamic_slice_in_dim(up_matrix, first, DB, 0)
            return carry + rounded(jnp.einsum("mtd,df->mtf", feat_cols, matrix_rows, preferred_element_type=jnp.float32)), None

        preact, _ = lax.scan(block_sum, jnp.zeros((MICRO, TOKENS, FF), jnp.float32), jnp.arange(N_DP, dtype=jnp.int32))
        back_hidden = (cotangent.astype(jnp.float32) * gelu_slope(preact)).astype(jnp.bfloat16)
        grad_up = jnp.einsum("mtd,mtf->df", features, back_hidden, preferred_element_type=jnp.float32)

        def tensor_sum(carry, index):
            first_col = index * F_DEV
            hidden_cols = lax.dynamic_slice_in_dim(back_hidden, first_col, F_DEV, 2)
            matrix_cols = lax.dynamic_slice_in_dim(up_matrix, first_col, F_DEV, 1)
            return carry + rounded(jnp.einsum("mtf,df->mtd", hidden_cols, matrix_cols, preferred_element_type=jnp.float32)), None

        input_grad, _ = lax.scan(tensor_sum, jnp.zeros((MICRO, TOKENS, D), jnp.float32), jnp.arange(N_TENSOR, dtype=jnp.int32))
        return input_grad.astype(jnp.bfloat16), grad_up.astype(jnp.bfloat16)

    input_grad, grad_up = lax.map(section_grads, (received, hid_cot, w_up))
    return jnp.roll(input_grad, -1, axis=0), grad_up
```

```python
import jax
import jax.numpy as jnp
from jax import lax
from jax.sharding import PartitionSpec as P

BLOCK = 128
CORES = 2


eps_scale = 1e-06
gelu_coef = 0.7978845608028654
cubic_coef = 0.044715


def from_behind(value, axis, steps):
    count = lax.axis_size(axis)
    pairs = [(source, (source + steps) % count) for source in range(count)]
    return lax.ppermute(value, axis, pairs)


def from_sibling(value):
    return lax.ppermute(value, "dp", [(d, d ^ 1) for d in range(lax.axis_size("dp"))])


def gelu_slope(preact):
    tanh_arg = gelu_coef * (preact + cubic_coef * preact * preact * preact)
    tangent = jnp.tanh(tanh_arg)
    return 0.5 * (1.0 + tangent) + 0.5 * preact * (1.0 - tangent * tangent) * gelu_coef * (
        1.0 + 3.0 * cubic_coef * preact * preact
    )


def exchange(value, axis, groups):
    return lax.all_to_all(value, axis, 0, 0, axis_index_groups=groups, tiled=False)


def gathered(value, axis, groups):
    return exchange(jnp.broadcast_to(value[None], (len(groups[0]), *value.shape)), axis, groups)


def dot(a, b, contract):
    return lax.dot_general(a, b, (contract, ((), ())), preferred_element_type=jnp.float32)


def local(x_prev, hid_cot, w_up):
    f32, bf16 = jnp.float32, jnp.bfloat16
    micro, own_rows, width = x_prev.shape[1:]
    n_dp, n_tensor = lax.axis_size("dp"), lax.axis_size("tensor")
    n_y = n_dp // CORES
    n_z = n_y
    n_x = n_tensor // n_z
    rows = micro * own_rows
    hidden = w_up.shape[2]
    half = hidden // CORES
    y_groups = [[y * CORES + c for y in range(n_y)] for c in range(CORES)]
    x_groups = [[z * n_x + x for x in range(n_x)] for z in range(n_z)]
    z_groups = [[z * n_x + x for z in range(n_z)] for x in range(n_x)]
    core = lax.axis_index("dp") % CORES

    blocks = x_prev[0].reshape(micro, own_rows, width // BLOCK, BLOCK)
    block_scale = (jnp.max(jnp.abs(blocks), axis=-1, keepdims=True) + eps_scale).astype(bf16).astype(f32)
    coded = (blocks / block_scale).astype(bf16)
    restored = (coded.astype(f32) * block_scale).astype(bf16).reshape(rows, width)
    received = from_behind(restored, "pipe", 1)

    cot = hid_cot[0].reshape(micro, n_x // CORES, own_rows, hidden).transpose(1, 0, 2, 3)
    cot = cot.reshape(n_x // CORES * rows, hidden)
    cot_own = lax.dynamic_slice_in_dim(cot, core * half, half, 1)
    cot_in = from_sibling(lax.dynamic_slice_in_dim(cot, (1 - core) * half, half, 1))
    cot_all = jnp.where(core == 0, jnp.concatenate([cot_own, cot_in]), jnp.concatenate([cot_in, cot_own]))

    w_own = lax.dynamic_slice_in_dim(w_up[0], core * half, half, 1)
    w_other = lax.dynamic_slice_in_dim(w_up[0], (1 - core) * half, half, 1)

    by_z = gathered(received, "tensor", z_groups)
    by_xz = gathered(by_z, "tensor", x_groups)
    features = by_xz.transpose(1, 0, 2, 3).reshape(n_z * n_x * rows, width)

    part_other = dot(features, w_other, ((1,), (0,))).astype(bf16)
    part_in = from_sibling(part_other)
    part_own = dot(features, w_own, ((1,), (0,))).astype(bf16)
    part = (part_own.astype(f32) + part_in.astype(f32)).astype(bf16)
    parts = exchange(part.reshape(n_y, n_x * rows, half), "dp", y_groups)
    preact = jnp.sum(parts.astype(f32), axis=0)
    back = (cot_all.astype(f32) * gelu_slope(preact)).astype(bf16)
    back_own = gathered(back, "dp", y_groups).reshape(n_z * n_x * rows, half)
    back_other = from_sibling(back_own)

    term = dot(back_own, w_own, ((1,), (1,))) + dot(back_other, w_other, ((1,), (1,)))
    term = term.astype(bf16).reshape(n_z, n_x, rows, width).transpose(1, 0, 2, 3)
    by_x = exchange(term, "tensor", x_groups)
    sum_x = jnp.sum(by_x.astype(f32), axis=0).astype(bf16)
    by_z = exchange(sum_x, "tensor", z_groups)
    back_input = jnp.sum(by_z.astype(f32), axis=0).astype(bf16).reshape(micro, own_rows, width)
    upstream = from_behind(back_input, "pipe", -1)

    grad_own = dot(features, back_own, ((0,), (0,))).astype(bf16)
    grad_other = dot(features, back_other, ((0,), (0,))).astype(bf16)
    grad = jnp.where(
        core == 0,
        jnp.concatenate([grad_own, grad_other], 1),
        jnp.concatenate([grad_other, grad_own], 1),
    )
    return (upstream[None], grad[None])


def solution(mesh):
    return jax.shard_map(
        local,
        mesh=mesh,
        in_specs=(
            P("pipe", None, "tensor", "dp"),
            P("pipe", None, "dp", "tensor"),
            P("pipe", "dp", "tensor"),
        ),
        out_specs=(P("pipe", None, "tensor", "dp"), P("pipe", "dp", "tensor")),
        check_vma=False,
    )
```

```python
import jax
import jax.numpy as jnp
from jax import lax
from jax.experimental import pallas as pl
from jax.experimental.pallas import tpu as pltpu
from jax.sharding import PartitionSpec as P

BLOCK = 128
CORES = 2
LAG = 18


eps_scale = 1e-06
gelu_coef = 0.7978845608028654
cubic_coef = 0.044715


def section_shift(value, steps):
    n_pipe = lax.axis_size("pipe")
    return lax.ppermute(value, "pipe", [(s, (s + steps) % n_pipe) for s in range(n_pipe)])


def from_sibling(value):
    return lax.ppermute(value, "dp", [(d, d ^ 1) for d in range(lax.axis_size("dp"))])


def gelu_slope(preact):
    tanh_arg = gelu_coef * (preact + cubic_coef * preact * preact * preact)
    tangent = jnp.tanh(tanh_arg)
    return 0.5 * (1.0 + tangent) + 0.5 * preact * (1.0 - tangent * tangent) * gelu_coef * (
        1.0 + 3.0 * cubic_coef * preact * preact
    )


def exchange(value, axis, groups):
    return lax.all_to_all(value, axis, 0, 0, axis_index_groups=groups, tiled=False)


def gathered(value, axis, groups):
    return exchange(jnp.broadcast_to(value[None], (len(groups[0]), *value.shape)), axis, groups)


def dot(a, b, contract):
    return lax.dot_general(a, b, (contract, ((), ())), preferred_element_type=jnp.float32)


def forward_kernel(core_ref, by_xz_ref, own_ref, other_ref, part_ref, feat_ref):
    f32, bf16 = jnp.float32, jnp.bfloat16
    n_x, n_zc, rows, _ = by_xz_ref.shape
    core = core_ref[0]

    @pl.when(pl.program_id(0) == 0)
    def _():
        for side in range(CORES):
            block = core if side == 0 else 1 - core
            for z in range(n_zc // CORES):
                piece = [by_xz_ref[x, z * CORES + block].astype(f32) for x in range(n_x)]
                feat_ref[side, pl.ds(z * n_x * rows, n_x * rows)] = jnp.concatenate(piece).astype(bf16)

    part = jnp.dot(feat_ref[0], own_ref[...], preferred_element_type=f32)
    part += jnp.dot(feat_ref[1], other_ref[...], preferred_element_type=f32)
    part_ref[...] = part.astype(bf16).reshape(part_ref.shape)


def forward(core, by_xz, w_own, w_other, tile):
    n_x, n_zc, rows, width = by_xz.shape
    hidden = w_own.shape[1]
    n_z = n_zc // CORES
    tokens = n_z * n_x * rows
    whole = lambda shape: pl.BlockSpec(shape, lambda j, _: (0,) * len(shape))
    weights = pl.BlockSpec((width, tile), lambda j, _: (0, j))
    return pl.pallas_call(
        forward_kernel,
        out_shape=(
            jax.ShapeDtypeStruct((n_z, n_x * rows, hidden), jnp.bfloat16),
            jax.ShapeDtypeStruct((CORES, tokens, width), jnp.bfloat16),
        ),
        grid_spec=pltpu.PrefetchScalarGridSpec(
            num_scalar_prefetch=1,
            grid=(hidden // tile,),
            in_specs=[whole(by_xz.shape), weights, weights],
            out_specs=(
                pl.BlockSpec((n_z, n_x * rows, tile), lambda j, _: (0, 0, j)),
                whole((CORES, tokens, width)),
            ),
        ),
        compiler_params=pltpu.CompilerParams(vmem_limit_bytes=40 * 2**20),
        cost_estimate=pl.CostEstimate(
            flops=2 * tokens * CORES * width * hidden, bytes_accessed=10 * 2**20, transcendentals=0
        ),
    )(core, by_xz, w_own, w_other)


def backward_kernel(core_ref, back_ref, own_ref, other_ref, term_ref):
    n_x, n_zc, rows, _ = term_ref.shape
    core = core_ref[0]
    for side, w_ref in enumerate((own_ref, other_ref)):
        block = core if side == 0 else 1 - core
        term = dot(back_ref[...], w_ref[...], ((1,), (1,)))
        for z in range(n_zc // CORES):
            for x in range(n_x):
                first = (z * n_x + x) * rows
                term_ref[x, z * CORES + block] = term[first : first + rows].astype(jnp.bfloat16)


def backward(core, back, w_own, w_other, n_z, n_x, tile):
    tokens, hidden = back.shape
    width = w_own.shape[0]
    rows = tokens // n_z // n_x
    weights = pl.BlockSpec((tile, hidden), lambda j, _: (j, 0))
    shape = (n_x, n_z * CORES, rows, width)
    return pl.pallas_call(
        backward_kernel,
        out_shape=jax.ShapeDtypeStruct(shape, jnp.bfloat16),
        grid_spec=pltpu.PrefetchScalarGridSpec(
            num_scalar_prefetch=1,
            grid=(width // tile,),
            in_specs=[pl.BlockSpec((tokens, hidden), lambda j, _: (0, 0)), weights, weights],
            out_specs=pl.BlockSpec((*shape[:3], tile), lambda j, _: (0, 0, 0, j)),
        ),
        compiler_params=pltpu.CompilerParams(vmem_limit_bytes=40 * 2**20),
        cost_estimate=pl.CostEstimate(
            flops=2 * tokens * CORES * width * hidden, bytes_accessed=8 * 2**20, transcendentals=0
        ),
    )(core, back, w_own, w_other)


def local(x_prev, hid_cot, w_up):
    f32, bf16 = jnp.float32, jnp.bfloat16
    micro, own_rows, width = x_prev.shape[1:]
    n_dp, n_tensor = lax.axis_size("dp"), lax.axis_size("tensor")
    n_y = n_dp // CORES
    n_z = n_y
    n_x = n_tensor // n_z
    tokens = n_tensor * own_rows
    hidden = w_up.shape[2]
    y_groups = [[y * CORES + c for y in range(n_y)] for c in range(CORES)]
    x_groups = [[z * n_x + x for x in range(n_x)] for z in range(n_z)]
    zc_groups = [
        [(y * CORES + c) * n_tensor + z * n_x + x for z in range(n_z) for c in range(CORES)]
        for y in range(n_y)
        for x in range(n_x)
    ]
    core = lax.axis_index("dp") % CORES
    core_list = core.reshape(1).astype(jnp.int32)
    mine = lambda value: lax.dynamic_index_in_dim(value, core, 0, False)
    siblings = lambda value: lax.dynamic_index_in_dim(value, 1 - core, 0, False)

    blocks = x_prev[0].reshape(micro, own_rows, width // BLOCK, BLOCK)
    block_scale = (jnp.max(jnp.abs(blocks), axis=-1, keepdims=True) + eps_scale).astype(bf16).astype(f32)
    coded = (blocks / block_scale).astype(bf16)
    restored = (coded.astype(f32) * block_scale).astype(bf16).reshape(micro, own_rows, width)
    received = section_shift(restored, 1)

    restored_c, cot = lax.optimization_barrier((restored, hid_cot[0]))
    cot_in = from_sibling(siblings(cot))
    cot_in, w_own = lax.optimization_barrier((cot_in, w_up[0]))
    w_other = from_sibling(w_own)
    cot_own = mine(cot)
    cot_all = jnp.where(core == 0, jnp.concatenate([cot_own, cot_in]), jnp.concatenate([cot_in, cot_own]))

    sent = jnp.broadcast_to(received[None], (n_z, micro, own_rows, width)).reshape(-1, own_rows, width)
    by_z = exchange(sent, ("dp", "tensor"), zc_groups)
    by_z = lax.fori_loop(0, (1 - core) * LAG, lambda i, v: jnp.maximum(v, -jnp.abs(v)), by_z)
    by_xz = gathered(by_z, "tensor", x_groups)
    part, features = forward(core_list, by_xz, w_own, w_other, 256)
    parts = exchange(part, "dp", y_groups)
    preact = jnp.sum(parts.astype(f32), axis=0)
    back = (cot_all.astype(f32) * gelu_slope(preact)).astype(bf16)
    back_all = gathered(back, "dp", y_groups).reshape(tokens, hidden)

    term = backward(core_list, back_all, w_own, w_other, n_z, n_x, 256)
    sum_x = jnp.sum(exchange(term, "tensor", x_groups).astype(f32), axis=0).astype(bf16)
    returned = exchange(sum_x, ("dp", "tensor"), zc_groups).reshape(n_z, micro, own_rows, width)
    back_input = jnp.sum(returned.astype(f32), axis=0).astype(bf16)
    upstream = section_shift(back_input, -1)

    back_late, _ = lax.optimization_barrier((back_all, term))
    grad_other = dot(features[1], back_late, ((0,), (0,))).astype(bf16)
    grad_other, _ = lax.optimization_barrier((grad_other, back_input))
    grad_in = from_sibling(grad_other)
    grad = (dot(features[0], back_late, ((0,), (0,))) + grad_in.astype(f32)).astype(bf16)
    upstream, grad = lax.optimization_barrier((upstream, grad))
    return (upstream[None], grad[None])


def solution(mesh):
    return jax.shard_map(
        local,
        mesh=mesh,
        in_specs=(
            P("pipe", None, "tensor", "dp"),
            P("pipe", None, "dp", "tensor"),
            P("pipe", "dp", "tensor"),
        ),
        out_specs=(P("pipe", None, "tensor", "dp"), P("pipe", "dp", "tensor")),
        check_vma=False,
    )
```

```python
import jax
import jax.numpy as jnp
from jax import lax
from jax.experimental import pallas as pl
from jax.experimental.pallas import tpu as pltpu
from jax.sharding import PartitionSpec as P

BLOCK = 128
CORES = 2
LAG = 18


eps_scale = 1e-06
gelu_coef = 0.7978845608028654
cubic_coef = 0.044715


def section_shift(value, steps):
    n_pipe = lax.axis_size("pipe")
    return lax.ppermute(value, "pipe", [(s, (s + steps) % n_pipe) for s in range(n_pipe)])


def from_sibling(value):
    return lax.ppermute(value, "dp", [(d, d ^ 1) for d in range(lax.axis_size("dp"))])


def gelu_slope(preact):
    tanh_arg = gelu_coef * (preact + cubic_coef * preact * preact * preact)
    tangent = jnp.tanh(tanh_arg)
    return 0.5 * (1.0 + tangent) + 0.5 * preact * (1.0 - tangent * tangent) * gelu_coef * (
        1.0 + 3.0 * cubic_coef * preact * preact
    )


def exchange(value, axis, groups):
    return lax.all_to_all(value, axis, 0, 0, axis_index_groups=groups, tiled=False)


def gathered(value, axis, groups):
    return exchange(jnp.broadcast_to(value[None], (len(groups[0]), *value.shape)), axis, groups)


def dot(a, b, contract):
    return lax.dot_general(a, b, (contract, ((), ())), preferred_element_type=jnp.float32)


def forward_kernel(core_ref, by_xz_ref, own_ref, other_ref, part_ref, feat_ref):
    f32, bf16 = jnp.float32, jnp.bfloat16
    n_x, n_zc, rows, _ = by_xz_ref.shape
    core = core_ref[0]

    @pl.when(pl.program_id(0) == 0)
    def _():
        for side in range(CORES):
            block = core if side == 0 else 1 - core
            for z in range(n_zc // CORES):
                piece = [by_xz_ref[x, z * CORES + block].astype(f32) for x in range(n_x)]
                feat_ref[side, pl.ds(z * n_x * rows, n_x * rows)] = jnp.concatenate(piece).astype(bf16)

    part = jnp.dot(feat_ref[0], own_ref[...], preferred_element_type=f32)
    part += jnp.dot(feat_ref[1], other_ref[...], preferred_element_type=f32)
    part_ref[...] = part.astype(bf16).reshape(part_ref.shape)


def forward(core, by_xz, w_own, w_other, tile):
    n_x, n_zc, rows, width = by_xz.shape
    hidden = w_own.shape[1]
    n_z = n_zc // CORES
    tokens = n_z * n_x * rows
    whole = lambda shape: pl.BlockSpec(shape, lambda j, _: (0,) * len(shape))
    weights = pl.BlockSpec((width, tile), lambda j, _: (0, j))
    return pl.pallas_call(
        forward_kernel,
        out_shape=(
            jax.ShapeDtypeStruct((n_z, n_x * rows, hidden), jnp.bfloat16),
            jax.ShapeDtypeStruct((CORES, tokens, width), jnp.bfloat16),
        ),
        grid_spec=pltpu.PrefetchScalarGridSpec(
            num_scalar_prefetch=1,
            grid=(hidden // tile,),
            in_specs=[whole(by_xz.shape), weights, weights],
            out_specs=(
                pl.BlockSpec((n_z, n_x * rows, tile), lambda j, _: (0, 0, j)),
                whole((CORES, tokens, width)),
            ),
        ),
        compiler_params=pltpu.CompilerParams(vmem_limit_bytes=16 * 2**20),
        cost_estimate=pl.CostEstimate(
            flops=2 * tokens * CORES * width * hidden, bytes_accessed=10 * 2**20, transcendentals=0
        ),
    )(core, by_xz, w_own, w_other)


def backward_kernel(core_ref, back_ref, own_ref, other_ref, term_ref):
    n_x, n_zc, rows, _ = term_ref.shape
    core = core_ref[0]
    for side, w_ref in enumerate((own_ref, other_ref)):
        block = core if side == 0 else 1 - core
        term = dot(back_ref[...], w_ref[...], ((1,), (1,)))
        for z in range(n_zc // CORES):
            for x in range(n_x):
                first = (z * n_x + x) * rows
                term_ref[x, z * CORES + block] = term[first : first + rows].astype(jnp.bfloat16)


def backward(core, back, w_own, w_other, n_z, n_x, tile):
    tokens, hidden = back.shape
    width = w_own.shape[0]
    rows = tokens // n_z // n_x
    weights = pl.BlockSpec((tile, hidden), lambda j, _: (j, 0))
    shape = (n_x, n_z * CORES, rows, width)
    return pl.pallas_call(
        backward_kernel,
        out_shape=jax.ShapeDtypeStruct(shape, jnp.bfloat16),
        grid_spec=pltpu.PrefetchScalarGridSpec(
            num_scalar_prefetch=1,
            grid=(width // tile,),
            in_specs=[pl.BlockSpec((tokens, hidden), lambda j, _: (0, 0)), weights, weights],
            out_specs=pl.BlockSpec((*shape[:3], tile), lambda j, _: (0, 0, 0, j)),
        ),
        compiler_params=pltpu.CompilerParams(vmem_limit_bytes=16 * 2**20),
        cost_estimate=pl.CostEstimate(
            flops=2 * tokens * CORES * width * hidden, bytes_accessed=8 * 2**20, transcendentals=0
        ),
    )(core, back, w_own, w_other)


def local(x_prev, hid_cot, w_up):
    f32, bf16 = jnp.float32, jnp.bfloat16
    micro, own_rows, width = x_prev.shape[1:]
    n_dp, n_tensor = lax.axis_size("dp"), lax.axis_size("tensor")
    n_y = n_dp // CORES
    n_z = n_y
    n_x = n_tensor // n_z
    tokens = n_tensor * own_rows
    hidden = w_up.shape[2]
    y_groups = [[y * CORES + c for y in range(n_y)] for c in range(CORES)]
    x_groups = [[z * n_x + x for x in range(n_x)] for z in range(n_z)]
    zc_groups = [
        [(y * CORES + c) * n_tensor + z * n_x + x for z in range(n_z) for c in range(CORES)]
        for y in range(n_y)
        for x in range(n_x)
    ]
    core = lax.axis_index("dp") % CORES
    core_list = core.reshape(1).astype(jnp.int32)
    mine = lambda value: lax.dynamic_index_in_dim(value, core, 0, False)
    siblings = lambda value: lax.dynamic_index_in_dim(value, 1 - core, 0, False)

    blocks = x_prev[0].reshape(micro, own_rows, width // BLOCK, BLOCK)
    block_scale = (jnp.max(jnp.abs(blocks), axis=-1, keepdims=True) + eps_scale).astype(bf16).astype(f32)
    coded = (blocks / block_scale).astype(bf16)
    restored = (coded.astype(f32) * block_scale).astype(bf16).reshape(micro, own_rows, width)
    received = section_shift(restored, 1)

    sent = jnp.broadcast_to(received[None], (n_z, micro, own_rows, width)).reshape(-1, own_rows, width)
    sent, w_own, cot = lax.optimization_barrier((sent, w_up[0], hid_cot[0]))
    w_other = from_sibling(w_own)
    cot_in = from_sibling(siblings(cot))
    cot_own = mine(cot)
    cot_all = jnp.where(core == 0, jnp.concatenate([cot_own, cot_in]), jnp.concatenate([cot_in, cot_own]))

    by_z = exchange(sent, ("dp", "tensor"), zc_groups)
    by_z, w_other, cot_all = lax.optimization_barrier((by_z, w_other, cot_all))
    by_z = lax.fori_loop(0, (1 - core) * LAG, lambda i, v: jnp.maximum(v, -jnp.abs(v)), by_z)
    by_xz = gathered(by_z, "tensor", x_groups)
    part, features = forward(core_list, by_xz, w_own, w_other, 256)
    parts = exchange(part, "dp", y_groups)
    preact = jnp.sum(parts.astype(f32), axis=0)
    back = (cot_all.astype(f32) * gelu_slope(preact)).astype(bf16)
    back_all = gathered(back, "dp", y_groups).reshape(tokens, hidden)

    term = backward(core_list, back_all, w_own, w_other, n_z, n_x, 256)
    sum_x = jnp.sum(exchange(term, "tensor", x_groups).astype(f32), axis=0).astype(bf16)

    back_late, _ = lax.optimization_barrier((back_all, term))
    grad_in = []
    for piece in jnp.split(features[1], 3, axis=1):
        grad_in.append(from_sibling(dot(piece, back_late, ((0,), (0,))).astype(bf16)))

    returned = exchange(sum_x, ("dp", "tensor"), zc_groups).reshape(n_z, micro, own_rows, width)
    back_input = jnp.sum(returned.astype(f32), axis=0).astype(bf16)
    upstream = section_shift(back_input, -1)
    grad = dot(features[0], back_late, ((0,), (0,))) + jnp.concatenate(grad_in).astype(f32)
    upstream, grad = lax.optimization_barrier((upstream, grad.astype(bf16)))
    return (upstream[None], grad[None])


def solution(mesh):
    return jax.shard_map(
        local,
        mesh=mesh,
        in_specs=(
            P("pipe", None, "tensor", "dp"),
            P("pipe", None, "dp", "tensor"),
            P("pipe", "dp", "tensor"),
        ),
        out_specs=(P("pipe", None, "tensor", "dp"), P("pipe", "dp", "tensor")),
        check_vma=False,
    )
```

```python
import jax
import jax.numpy as jnp
from jax import lax
from jax.experimental import pallas as pl
from jax.experimental.pallas import tpu as pltpu
from jax.sharding import PartitionSpec as P

BLOCK = 128
CORES = 2
LAG = 18
TILE = 512
ROWS = 256


eps_scale = 1e-06
gelu_coef = 0.7978845608028654
cubic_coef = 0.044715


def section_shift(value, steps):
    n_pipe = lax.axis_size("pipe")
    return lax.ppermute(value, "pipe", [(s, (s + steps) % n_pipe) for s in range(n_pipe)])


def from_sibling(value):
    return lax.ppermute(value, "dp", [(d, d ^ 1) for d in range(lax.axis_size("dp"))])


def gelu_slope(preact):
    tanh_arg = gelu_coef * (preact + cubic_coef * preact * preact * preact)
    tangent = jnp.tanh(tanh_arg)
    return 0.5 * (1.0 + tangent) + 0.5 * preact * (1.0 - tangent * tangent) * gelu_coef * (
        1.0 + 3.0 * cubic_coef * preact * preact
    )


def exchange(value, axis, groups):
    return lax.all_to_all(value, axis, 0, 0, axis_index_groups=groups, tiled=False)


def gathered(value, axis, groups):
    return exchange(jnp.broadcast_to(value[None], (len(groups[0]), *value.shape)), axis, groups)


def dot(a, b, contract):
    return lax.dot_general(a, b, (contract, ((), ())), preferred_element_type=jnp.float32)


def forward_kernel(core_ref, by_xz_ref, own_ref, other_ref, part_ref, feat_ref):
    f32, bf16 = jnp.float32, jnp.bfloat16
    n_x, n_zc, rows, _ = by_xz_ref.shape
    for side in range(CORES):
        block = core_ref[0] if side == 0 else 1 - core_ref[0]
        for z in range(n_zc // CORES):
            piece = [by_xz_ref[x, z * CORES + block].astype(f32) for x in range(n_x)]
            feat_ref[side, pl.ds(z * n_x * rows, n_x * rows)] = jnp.concatenate(piece).astype(bf16)
    for first in range(0, part_ref.shape[2], TILE):
        columns = pl.ds(first, TILE)
        part = jnp.dot(feat_ref[0], own_ref[:, columns], preferred_element_type=f32)
        part += jnp.dot(feat_ref[1], other_ref[:, columns], preferred_element_type=f32)
        part_ref[:, :, columns] = part.astype(bf16).reshape(*part_ref.shape[:2], TILE)


def forward(core, by_xz, w_own, w_other):
    n_x, n_zc, rows, width = by_xz.shape
    hidden = w_own.shape[1]
    n_z = n_zc // CORES
    tokens = n_z * n_x * rows
    vmem = pl.BlockSpec(memory_space=pltpu.VMEM)
    return pl.pallas_call(
        forward_kernel,
        out_shape=(
            jax.ShapeDtypeStruct((n_z, n_x * rows, hidden), jnp.bfloat16),
            jax.ShapeDtypeStruct((CORES, tokens, width), jnp.bfloat16),
        ),
        in_specs=[pl.BlockSpec(memory_space=pltpu.SMEM), vmem, vmem, vmem],
        out_specs=(vmem, vmem),
        compiler_params=pltpu.CompilerParams(vmem_limit_bytes=20 * 2**20),
        cost_estimate=pl.CostEstimate(
            flops=2 * tokens * CORES * width * hidden, bytes_accessed=10 * 2**20, transcendentals=0
        ),
    )(core, by_xz, w_own, w_other)


def backward_kernel(core_ref, back_ref, own_ref, other_ref, term_ref):
    n_x, n_zc, rows, width = term_ref.shape
    for side, w_ref in enumerate((own_ref, other_ref)):
        block = core_ref[0] if side == 0 else 1 - core_ref[0]
        for tile in range(0, width, ROWS):
            term = dot(back_ref[...], w_ref[pl.ds(tile, ROWS)], ((1,), (1,)))
            for z in range(n_zc // CORES):
                for x in range(n_x):
                    first = (z * n_x + x) * rows
                    piece = term[first : first + rows].astype(jnp.bfloat16)
                    term_ref[x, z * CORES + block, :, pl.ds(tile, ROWS)] = piece


def backward(core, back, w_own, w_other, n_z, n_x):
    tokens, hidden = back.shape
    width = w_own.shape[0]
    vmem = pl.BlockSpec(memory_space=pltpu.VMEM)
    return pl.pallas_call(
        backward_kernel,
        out_shape=jax.ShapeDtypeStruct((n_x, n_z * CORES, tokens // n_z // n_x, width), jnp.bfloat16),
        in_specs=[pl.BlockSpec(memory_space=pltpu.SMEM), vmem, vmem, vmem],
        out_specs=vmem,
        compiler_params=pltpu.CompilerParams(vmem_limit_bytes=20 * 2**20),
        cost_estimate=pl.CostEstimate(
            flops=2 * tokens * CORES * width * hidden, bytes_accessed=8 * 2**20, transcendentals=0
        ),
    )(core, back, w_own, w_other)


def local(x_prev, hid_cot, w_up):
    f32, bf16 = jnp.float32, jnp.bfloat16
    micro, own_rows, width = x_prev.shape[1:]
    n_dp, n_tensor = lax.axis_size("dp"), lax.axis_size("tensor")
    n_y = n_dp // CORES
    n_z = n_y
    n_x = n_tensor // n_z
    tokens = n_tensor * own_rows
    hidden = w_up.shape[2]
    y_groups = [[y * CORES + c for y in range(n_y)] for c in range(CORES)]
    x_groups = [[z * n_x + x for x in range(n_x)] for z in range(n_z)]
    zc_groups = [
        [(y * CORES + c) * n_tensor + z * n_x + x for z in range(n_z) for c in range(CORES)]
        for y in range(n_y)
        for x in range(n_x)
    ]
    core = lax.axis_index("dp") % CORES
    core_list = core.reshape(1).astype(jnp.int32)
    mine = lambda value: lax.dynamic_index_in_dim(value, core, 0, False)
    siblings = lambda value: lax.dynamic_index_in_dim(value, 1 - core, 0, False)

    blocks = x_prev[0].reshape(micro, own_rows, width // BLOCK, BLOCK)
    block_scale = (jnp.max(jnp.abs(blocks), axis=-1, keepdims=True) + eps_scale).astype(bf16).astype(f32)
    coded = (blocks / block_scale).astype(bf16)
    restored = (coded.astype(f32) * block_scale).astype(bf16).reshape(micro, own_rows, width)
    received = section_shift(restored, 1)

    sent = jnp.broadcast_to(received[None], (n_z, micro, own_rows, width)).reshape(-1, own_rows, width)
    sent, w_own, cot = lax.optimization_barrier((sent, w_up[0], hid_cot[0]))
    w_other = from_sibling(w_own)
    cot_in = from_sibling(siblings(cot))
    cot_own = mine(cot)
    cot_all = jnp.where(core == 0, jnp.concatenate([cot_own, cot_in]), jnp.concatenate([cot_in, cot_own]))

    by_z = exchange(sent, ("dp", "tensor"), zc_groups)
    by_z, w_other, cot_all = lax.optimization_barrier((by_z, w_other, cot_all))
    by_z = lax.fori_loop(0, (1 - core) * LAG, lambda i, v: jnp.maximum(v, -jnp.abs(v)), by_z)
    by_xz = gathered(by_z, "tensor", x_groups)
    part, features = forward(core_list, by_xz, w_own, w_other)
    parts = exchange(part, "dp", y_groups)
    preact = jnp.sum(parts.astype(f32), axis=0)
    back = (cot_all.astype(f32) * gelu_slope(preact)).astype(bf16)
    back_all = gathered(back, "dp", y_groups).reshape(tokens, hidden)

    term = backward(core_list, back_all, w_own, w_other, n_z, n_x)
    sum_x = jnp.sum(exchange(term, "tensor", x_groups).astype(f32), axis=0).astype(bf16)

    back_late, _ = lax.optimization_barrier((back_all, term))
    grad_in = []
    for piece in jnp.split(features[1], 3, axis=1):
        grad_in.append(from_sibling(dot(piece, back_late, ((0,), (0,))).astype(bf16)))

    returned = exchange(sum_x, ("dp", "tensor"), zc_groups).reshape(n_z, micro, own_rows, width)
    back_input = jnp.sum(returned.astype(f32), axis=0).astype(bf16)
    upstream = section_shift(back_input, -1)
    grad = dot(features[0], back_late, ((0,), (0,))) + jnp.concatenate(grad_in).astype(f32)
    upstream, grad = lax.optimization_barrier((upstream, grad.astype(bf16)))
    return (upstream[None], grad[None])


def solution(mesh):
    return jax.shard_map(
        local,
        mesh=mesh,
        in_specs=(
            P("pipe", None, "tensor", "dp"),
            P("pipe", None, "dp", "tensor"),
            P("pipe", "dp", "tensor"),
        ),
        out_specs=(P("pipe", None, "tensor", "dp"), P("pipe", "dp", "tensor")),
        check_vma=False,
    )
```

```python
import jax
import jax.numpy as jnp
from jax import lax
from jax.experimental import pallas as pl
from jax.experimental.pallas import tpu as pltpu
from jax.sharding import PartitionSpec as P

BLOCK = 128
CORES = 2
LAG = 18
TILE = 512
ROWS = 256


eps_scale = 1e-06
gelu_coef = 0.7978845608028654
cubic_coef = 0.044715


def section_shift(value, steps):
    n_pipe = lax.axis_size("pipe")
    return lax.ppermute(value, "pipe", [(s, (s + steps) % n_pipe) for s in range(n_pipe)])


def from_sibling(value):
    return lax.ppermute(value, "dp", [(d, d ^ 1) for d in range(lax.axis_size("dp"))])


def gelu_slope(preact):
    tanh_arg = gelu_coef * (preact + cubic_coef * preact * preact * preact)
    tangent = jnp.tanh(tanh_arg)
    return 0.5 * (1.0 + tangent) + 0.5 * preact * (1.0 - tangent * tangent) * gelu_coef * (
        1.0 + 3.0 * cubic_coef * preact * preact
    )


def exchange(value, axis, groups):
    return lax.all_to_all(value, axis, 0, 0, axis_index_groups=groups, tiled=False)


def gathered(value, axis, groups):
    return exchange(jnp.broadcast_to(value[None], (len(groups[0]), *value.shape)), axis, groups)


def dot(a, b, contract):
    return lax.dot_general(a, b, (contract, ((), ())), preferred_element_type=jnp.float32)


def forward_kernel(core_ref, by_xz_ref, own_ref, other_ref, part_ref, feat_ref):
    f32, bf16 = jnp.float32, jnp.bfloat16
    n_x, n_zc, rows, _ = by_xz_ref.shape
    for side in range(CORES):
        block = core_ref[0] if side == 0 else 1 - core_ref[0]
        for z in range(n_zc // CORES):
            piece = [by_xz_ref[x, z * CORES + block].astype(f32) for x in range(n_x)]
            feat_ref[side, pl.ds(z * n_x * rows, n_x * rows)] = jnp.concatenate(piece).astype(bf16)
    for first in range(0, part_ref.shape[2], TILE):
        columns = pl.ds(first, TILE)
        part = jnp.dot(feat_ref[0], own_ref[:, columns], preferred_element_type=f32)
        part += jnp.dot(feat_ref[1], other_ref[:, columns], preferred_element_type=f32)
        part_ref[:, :, columns] = part.astype(bf16).reshape(*part_ref.shape[:2], TILE)


def forward(core, by_xz, w_own, w_other):
    n_x, n_zc, rows, width = by_xz.shape
    hidden = w_own.shape[1]
    n_z = n_zc // CORES
    tokens = n_z * n_x * rows
    vmem = pl.BlockSpec(memory_space=pltpu.VMEM)
    return pl.pallas_call(
        forward_kernel,
        out_shape=(
            jax.ShapeDtypeStruct((n_z, n_x * rows, hidden), jnp.bfloat16),
            jax.ShapeDtypeStruct((CORES, tokens, width), jnp.bfloat16),
        ),
        in_specs=[pl.BlockSpec(memory_space=pltpu.SMEM), vmem, vmem, vmem],
        out_specs=(vmem, vmem),
        compiler_params=pltpu.CompilerParams(vmem_limit_bytes=20 * 2**20),
        cost_estimate=pl.CostEstimate(
            flops=2 * tokens * CORES * width * hidden, bytes_accessed=10 * 2**20, transcendentals=0
        ),
    )(core, by_xz, w_own, w_other)


def backward_kernel(core_ref, back_ref, own_ref, other_ref, term_ref):
    n_x, n_zc, rows, width = term_ref.shape
    for side, w_ref in enumerate((own_ref, other_ref)):
        block = core_ref[0] if side == 0 else 1 - core_ref[0]
        for tile in range(0, width, ROWS):
            term = dot(back_ref[...], w_ref[pl.ds(tile, ROWS)], ((1,), (1,)))
            for z in range(n_zc // CORES):
                for x in range(n_x):
                    first = (z * n_x + x) * rows
                    piece = term[first : first + rows].astype(jnp.bfloat16)
                    term_ref[x, z * CORES + block, :, pl.ds(tile, ROWS)] = piece


def backward(core, back, w_own, w_other, n_z, n_x):
    tokens, hidden = back.shape
    width = w_own.shape[0]
    vmem = pl.BlockSpec(memory_space=pltpu.VMEM)
    return pl.pallas_call(
        backward_kernel,
        out_shape=jax.ShapeDtypeStruct((n_x, n_z * CORES, tokens // n_z // n_x, width), jnp.bfloat16),
        in_specs=[pl.BlockSpec(memory_space=pltpu.SMEM), vmem, vmem, vmem],
        out_specs=vmem,
        compiler_params=pltpu.CompilerParams(vmem_limit_bytes=20 * 2**20),
        cost_estimate=pl.CostEstimate(
            flops=2 * tokens * CORES * width * hidden, bytes_accessed=8 * 2**20, transcendentals=0
        ),
    )(core, back, w_own, w_other)


def sum_kernel(parts_ref, sum_ref):
    total = parts_ref[0].astype(jnp.float32)
    for part in range(1, parts_ref.shape[0]):
        total += parts_ref[part].astype(jnp.float32)
    sum_ref[...] = total.astype(jnp.bfloat16)


def sum_parts(parts):
    vmem = pl.BlockSpec(memory_space=pltpu.VMEM)
    return pl.pallas_call(
        sum_kernel,
        out_shape=jax.ShapeDtypeStruct(parts.shape[1:], parts.dtype),
        in_specs=[vmem],
        out_specs=vmem,
        compiler_params=pltpu.CompilerParams(vmem_limit_bytes=16 * 2**20),
        cost_estimate=pl.CostEstimate(flops=parts.size, bytes_accessed=2 * parts.size, transcendentals=0),
    )(parts)


def local(x_prev, hid_cot, w_up):
    f32, bf16 = jnp.float32, jnp.bfloat16
    micro, own_rows, width = x_prev.shape[1:]
    n_dp, n_tensor = lax.axis_size("dp"), lax.axis_size("tensor")
    n_y = n_dp // CORES
    n_z = n_y
    n_x = n_tensor // n_z
    tokens = n_tensor * own_rows
    hidden = w_up.shape[2]
    y_groups = [[y * CORES + c for y in range(n_y)] for c in range(CORES)]
    x_groups = [[z * n_x + x for x in range(n_x)] for z in range(n_z)]
    zc_groups = [
        [(y * CORES + c) * n_tensor + z * n_x + x for z in range(n_z) for c in range(CORES)]
        for y in range(n_y)
        for x in range(n_x)
    ]
    core = lax.axis_index("dp") % CORES
    core_list = core.reshape(1).astype(jnp.int32)
    mine = lambda value: lax.dynamic_index_in_dim(value, core, 0, False)
    siblings = lambda value: lax.dynamic_index_in_dim(value, 1 - core, 0, False)

    blocks = x_prev[0].reshape(micro, own_rows, width // BLOCK, BLOCK)
    block_scale = (jnp.max(jnp.abs(blocks), axis=-1, keepdims=True) + eps_scale).astype(bf16).astype(f32)
    coded = (blocks / block_scale).astype(bf16)
    restored = (coded.astype(f32) * block_scale).astype(bf16).reshape(micro, own_rows, width)
    received = section_shift(restored, 1)

    sent = jnp.broadcast_to(received[None], (n_z, micro, own_rows, width)).reshape(-1, own_rows, width)
    sent, w_own, cot = lax.optimization_barrier((sent, w_up[0], hid_cot[0]))
    w_other = from_sibling(w_own)
    cot_in = from_sibling(siblings(cot))
    cot_own = mine(cot)
    cot_all = jnp.where(core == 0, jnp.concatenate([cot_own, cot_in]), jnp.concatenate([cot_in, cot_own]))

    by_z = exchange(sent, ("dp", "tensor"), zc_groups)
    by_z, w_other, cot_all = lax.optimization_barrier((by_z, w_other, cot_all))
    by_z = lax.fori_loop(0, (1 - core) * LAG, lambda i, v: jnp.maximum(v, -jnp.abs(v)), by_z)
    by_xz = gathered(by_z, "tensor", x_groups)
    part, features = forward(core_list, by_xz, w_own, w_other)
    parts = exchange(part, "dp", y_groups)
    preact = jnp.sum(parts.astype(f32), axis=0)
    back = (cot_all.astype(f32) * gelu_slope(preact)).astype(bf16)
    back_all = gathered(back, "dp", y_groups).reshape(tokens, hidden)

    term = backward(core_list, back_all, w_own, w_other, n_z, n_x)
    sum_x = sum_parts(exchange(term, "tensor", x_groups))

    back_late, _ = lax.optimization_barrier((back_all, term))
    grad_in = []
    for piece in jnp.split(features[1], 3, axis=1):
        grad_in.append(from_sibling(dot(piece, back_late, ((0,), (0,))).astype(bf16)))

    returned = exchange(sum_x, ("dp", "tensor"), zc_groups).reshape(n_z, micro, own_rows, width)
    back_input = jnp.sum(returned.astype(f32), axis=0).astype(bf16)
    upstream = section_shift(back_input, -1)
    grad = dot(features[0], back_late, ((0,), (0,))) + jnp.concatenate(grad_in).astype(f32)
    upstream, grad = lax.optimization_barrier((upstream, grad.astype(bf16)))
    return (upstream[None], grad[None])


def solution(mesh):
    return jax.shard_map(
        local,
        mesh=mesh,
        in_specs=(
            P("pipe", None, "tensor", "dp"),
            P("pipe", None, "dp", "tensor"),
            P("pipe", "dp", "tensor"),
        ),
        out_specs=(P("pipe", None, "tensor", "dp"), P("pipe", "dp", "tensor")),
        check_vma=False,
    )
```
